512 devices in a mesh: frame: 16 (over z, core), tok: 32 (over y, x).
Axes of the slice: x: 4, y: 8, z: 8, core: 2. Of those that a mesh axis runs over, the one named last changes fastest.
Arguments:
- latents: bfloat16 [64, 1024, 3072], P('frame', 'tok'), may hold values from -3 to 3
- queries: bfloat16 [64, 1024, 3072], P('frame', 'tok')
- keys: bfloat16 [64, 1024, 3072], P('frame', 'tok')
- values: bfloat16 [64, 1024, 3072], P('frame', 'tok'), may hold values from -48 to 48
- levels: int32 [64], P('frame'), may hold values from 0 to 127, as said below
- reach: int32 [64], P('frame'), may hold values from 0 to 2, as said below
- gates: bfloat16 [128, 3072], P('frame'), may hold values from 0.099609375 to 1.8984375
- steps_table: float32 [128], P('frame'), may hold values from 0.25 to 1
- fresh: bfloat16 [1024, 3072], P('tok'), may hold values from -6 to 6
Outputs:
- updated: bfloat16 [64, 1024, 3072], P('frame', 'tok')
- next_queue: bfloat16 [64, 1024, 3072], P('frame', 'tok')
The draws below stay inside these ranges and needn't reach their ends.
Inputs may be any that keep to these rules, and one draw needn't show every extreme that they name: Frame f's level is 2 f or 2 f + 1, so levels rise along the queue by 1, 2 or 3; frame 0 has level 0 and the last frame level 127. `reach`: the last frame's window is exactly 2.
All inputs are finite; a program needn't handle non-finite values.
Results may differ from the reference program's by a relative error of at most 0.0036.
Values may be sent and summed in bfloat16 or wider, within the bound.
A program may use at most 64 MiB of HBM per device.

```python
import math
import jax
import jax.numpy as jnp
from jax import lax

D = 3072
HEADS = 24
HEAD_DIM = 128
TOKENS_FRAME = 1024
REACH = 2
FRAMES = 64
LEVELS = 128


def shared_keys(key):
    return jax.random.normal(key, (FRAMES, TOKENS_FRAME, D), jnp.float32)


def draw_keys(key, part):
    base = shared_keys(key)
    return base.astype(jnp.bfloat16)


def draw_queries(key, part):
    key = jax.random.fold_in(key, 12)
    first = jax.random.fold_in(key, 0)
    result = jax.random.normal(first, (FRAMES, TOKENS_FRAME, D), jnp.float32)
    return result.astype(jnp.bfloat16)


def draw_levels(key, part):
    key = jax.random.fold_in(key, 21)
    extra = jax.random.randint(key, (FRAMES,), 0, 2)
    extra = extra.at[0].set(0).at[FRAMES - 1].set(1)
    return (2 * jnp.arange(FRAMES, dtype=jnp.int32) + extra).astype(jnp.int32)


def draw_reach(key, part):
    key = jax.random.fold_in(key, 31)
    windows = jax.random.randint(key, (FRAMES,), 0, REACH + 1)
    return windows.at[FRAMES - 1].set(REACH).astype(jnp.int32)


def block_scale(rng, extent, cuts, least, high):
    level = 1.0
    for position, shards_of in cuts:
        heights = jax.random.uniform(jax.random.fold_in(jax.random.fold_in(rng, 6), position), (shards_of,), jnp.float32, least / len(cuts), high / len(cuts))
        level = level * jnp.repeat(jnp.exp(heights), extent[position] // shards_of).reshape((-1,) + (1,) * (len(extent) - 1 - position))
    return level


def scatter_about(rng, dims, deviation, most, cuts=(), held_as=jnp.bfloat16):
    array = jax.random.normal(rng, dims, jnp.float32) * deviation
    if len(cuts) > 0:
        array = block_scale(rng, dims, cuts, -0.22, 0.18) * array
    return jnp.clip(array, min=-most, max=most).astype(held_as)


def setup_inputs(seed: int = 0) -> dict:
    arg_keys = jax.random.split(jax.random.key(seed), 10)
    latents = scatter_about(arg_keys[0], (FRAMES, TOKENS_FRAME, D), 0.5, 3.0, ((0, 16), (1, 32)))
    queries = draw_queries(jax.random.fold_in(arg_keys[9], 71), 0)
    keys = draw_keys(jax.random.fold_in(arg_keys[9], 71), 0)
    values = scatter_about(arg_keys[3], (FRAMES, TOKENS_FRAME, D), 8.0, 48.0, ((0, 16), (1, 32)))
    levels = draw_levels(jax.random.fold_in(arg_keys[9], 71), 0)
    reach = draw_reach(jax.random.fold_in(arg_keys[9], 71), 0)
    gates = jnp.clip(1.0 + 0.18 * jax.random.normal(arg_keys[6], (LEVELS, D), jnp.float32), 0.099609375, 1.8984375).astype(jnp.bfloat16)
    steps_table = jnp.clip(jnp.exp(math.log(1.0) - 1.3862944 * jax.random.uniform(arg_keys[7], (LEVELS,), jnp.float32) ** block_scale(arg_keys[7], (LEVELS,), ((0, 16),), -0.2, 0.2)), 0.25, 1.0)
    fresh = scatter_about(arg_keys[8], (TOKENS_FRAME, D), 1.0, 6.0, ((0, 32),))
    return dict(latents=latents, queries=queries, keys=keys, values=values, levels=levels, reach=reach, gates=gates, steps_table=steps_table, fresh=fresh)


masked_score = -1.0e30


def frame_attention(frame_index, queries, key_pad, val_pad, reach):
    scale = 1.0 / (HEAD_DIM ** 0.5)
    query_heads = queries[frame_index].astype(jnp.float32).reshape(TOKENS_FRAME, HEADS, HEAD_DIM)
    key_window = lax.dynamic_slice_in_dim(key_pad, frame_index, REACH + 1, 0).astype(jnp.float32)
    key_window = key_window.reshape(REACH + 1, TOKENS_FRAME, HEADS, HEAD_DIM)
    val_window = lax.dynamic_slice_in_dim(val_pad, frame_index, REACH + 1, 0).astype(jnp.float32)
    val_window = val_window.reshape(REACH + 1, TOKENS_FRAME, HEADS, HEAD_DIM)
    key_frames = frame_index - REACH + jnp.arange(REACH + 1, dtype=jnp.int32)
    allowed = (key_frames >= 0) & (key_frames >= frame_index - reach[frame_index])
    scores = jnp.einsum("thd,knhd->thkn", query_heads, key_window) * scale
    scores = jnp.where(allowed[None, None, :, None], scores, masked_score)
    top_score = jnp.max(scores, axis=(2, 3), keepdims=True)
    weights = jnp.exp(scores - top_score)
    running_sum = jnp.sum(weights, axis=(2, 3))
    rounded = lax.optimization_barrier(weights.astype(jnp.bfloat16)).astype(jnp.float32)
    numerator = jnp.einsum("thkn,knhd->thd", rounded, val_window)
    return (numerator / running_sum[..., None]).reshape(TOKENS_FRAME, D).astype(jnp.bfloat16)


def reference(latents, queries, keys, values, levels, reach, gates, steps_table, fresh):
    front = jnp.zeros((REACH, TOKENS_FRAME, D), jnp.bfloat16)
    key_pad = jnp.concatenate([front, keys], 0)
    val_pad = jnp.concatenate([front, values], 0)
    frame_ids = jnp.arange(FRAMES, dtype=jnp.int32)
    attn = lax.map(lambda frame_index: frame_attention(frame_index, queries, key_pad, val_pad, reach), frame_ids)
    gate_rows = gates[levels].astype(jnp.float32)
    step_sizes = steps_table[levels]
    updated = (latents.astype(jnp.float32) - step_sizes[:, None, None] * gate_rows[:, None, :] * attn.astype(jnp.float32)).astype(jnp.bfloat16)
    next_queue = jnp.concatenate([updated[1:], fresh[None]], 0)
    return updated, next_queue
```

```python
import functools
import math

import jax
import jax.numpy as jnp
from jax import lax
from jax.experimental import pallas as pl
from jax.experimental.pallas import tpu as pltpu
from jax.sharding import PartitionSpec as P

HEAD_DIM = 128
REACH = 2
FRAMES_HERE = 4
ROWS = 32
RING_Y = 8
RING_X = 4
GROUPS = 16
HEADS_HERE = 3
BLOCK = ROWS * RING_Y
FRAME_LEN = BLOCK * RING_X
WIDTH = RING_Y * HEADS_HERE * HEAD_DIM
SCALE = math.log2(math.e) / math.sqrt(HEAD_DIM)
MASKED = -1e30
MESH = pl.DeviceIdType.MESH
K, V, Q = 0, 1, 2
Y_STEPS = (4, 3, 5, 2, 6, 1, 7)
Y_ORDER = ((K, 0), (V, 0), (K, 1), (Q, 0), (V, 1), (K, 2), (Q, 1), (V, 2), (Q, 2))
K_RIGHT, K_LEFT, V_RIGHT, V_LEFT, K_RELAY, V_RELAY = range(6)
OWN, LEFT, RIGHT, FAR = range(4)


def kernel(
    latents, queries, keys, values, levels, reach, gates, steps_table, fresh,
    updated, next_queue,
    kbuf, vbuf, qbuf, obuf, attn, lat, gate, new, incoming,
    y_send, y_recv, y_here, x_send, x_recv, halo_send, halo_recv,
    o_send, o_recv, o_here, f_send, f_recv, in_sem,
):
    group = lax.axis_index("frame")
    place = lax.axis_index("tok")
    y, x = place // RING_X, place % RING_X
    bufs = {K: kbuf, V: vbuf, Q: qbuf}
    sources = {K: keys, V: values, Q: queries}

    def along_y(step):
        return (group, lax.rem(y + step, RING_Y) * RING_X + x)

    def along_x(step):
        return (group, y * RING_X + lax.rem(x + step + RING_X, RING_X))

    def along_frame(step):
        return (lax.rem(group + step + GROUPS, GROUPS), place)

    to_right, to_left = along_x(1), along_x(-1)
    next_group, last_group = along_frame(1), along_frame(-1)

    barrier = pltpu.get_barrier_semaphore()
    peers = [along_y(step) for step in range(1, RING_Y)] + [to_right, to_left, next_group, last_group]
    for peer in peers:
        pl.semaphore_signal(barrier, inc=1, device_id=peer, device_id_type=MESH)
    pl.semaphore_wait(barrier, len(peers))

    def columns(owner, head):
        return pl.ds(pl.multiple_of((owner * HEADS_HERE + head) * HEAD_DIM, HEAD_DIM), HEAD_DIM)

    def landing(array, head):
        rows = pl.multiple_of(y * ROWS, ROWS)
        if array == Q:
            return qbuf.at[head, :, pl.ds(rows, ROWS), :]
        rows = pl.multiple_of(x * BLOCK + y * ROWS, ROWS)
        return bufs[array].at[head, pl.ds(REACH, FRAMES_HERE), pl.ds(rows, ROWS), :]

    def y_copy(array, head, step):
        index = (array * HEADS_HERE + head) * RING_Y + step
        return pltpu.make_async_remote_copy(
            src_ref=sources[array].at[:, :, columns(lax.rem(y + step, RING_Y), head)],
            dst_ref=landing(array, head),
            send_sem=y_send.at[index],
            recv_sem=y_recv.at[index],
            device_id=along_y(step),
            device_id_type=MESH,
        )

    def y_own(array, head):
        return pltpu.make_async_copy(
            sources[array].at[:, :, columns(y, head)],
            landing(array, head),
            y_here.at[array * HEADS_HERE + head],
        )

    def block_rows(role):
        shift = {OWN: 0, LEFT: 3, RIGHT: 1, FAR: 2}[role]
        return pl.ds(pl.multiple_of(lax.rem(x + shift, RING_X) * BLOCK, BLOCK), BLOCK)

    def x_copy(head, kind):
        array = K if kind in (K_RIGHT, K_LEFT, K_RELAY) else V
        role = {K_RELAY: LEFT, V_RELAY: RIGHT}.get(kind, OWN)
        block = bufs[array].at[head, pl.ds(REACH, FRAMES_HERE), block_rows(role), :]
        return pltpu.make_async_remote_copy(
            src_ref=block,
            dst_ref=block,
            send_sem=x_send.at[head * 6 + kind],
            recv_sem=x_recv.at[head * 6 + kind],
            device_id=to_right if kind in (K_RIGHT, V_RIGHT, K_RELAY) else to_left,
            device_id_type=MESH,
        )

    def halo_copy(array, head, role):
        index = (array * HEADS_HERE + head) * 4 + role
        return pltpu.make_async_remote_copy(
            src_ref=bufs[array].at[head, pl.ds(FRAMES_HERE, REACH), block_rows(role), :],
            dst_ref=bufs[array].at[head, pl.ds(0, REACH), block_rows(role), :],
            send_sem=halo_send.at[index],
            recv_sem=halo_recv.at[index],
            device_id=next_group,
            device_id_type=MESH,
        )

    def o_copy(head, frame, step):
        index = (head * FRAMES_HERE + frame) * RING_Y + step
        rows = pl.ds(pl.multiple_of(lax.rem(y + step, RING_Y) * ROWS, ROWS), ROWS)
        return pltpu.make_async_remote_copy(
            src_ref=obuf.at[head, frame, rows, :],
            dst_ref=attn.at[frame, :, columns(y, head)],
            send_sem=o_send.at[index],
            recv_sem=o_recv.at[index],
            device_id=along_y(step),
            device_id_type=MESH,
        )

    def o_own(head, frame):
        rows = pl.ds(pl.multiple_of(y * ROWS, ROWS), ROWS)
        return pltpu.make_async_copy(
            obuf.at[head, frame, rows, :],
            attn.at[frame, :, columns(y, head)],
            o_here.at[head * FRAMES_HERE + frame],
        )

    frame_copy = pltpu.make_async_remote_copy(
        src_ref=new,
        dst_ref=incoming,
        send_sem=f_send.at[0],
        recv_sem=f_recv.at[0],
        device_id=last_group,
        device_id_type=MESH,
    )

    for array, head in Y_ORDER:
        for step in Y_STEPS:
            y_copy(array, head, step).start()
        y_own(array, head).start()
    lat_copy = pltpu.make_async_copy(latents, lat, in_sem.at[0])
    gate_copy = pltpu.make_async_copy(gates, gate, in_sem.at[1])
    lat_copy.start()
    gate_copy.start()

    def arrive(array, head):
        for step in Y_STEPS:
            y_copy(array, head, step).wait_recv()
        y_own(array, head).wait()

    def first(array, head):
        arrive(array, head)
        x_copy(head, K_RIGHT if array == K else V_RIGHT).start()
        x_copy(head, K_LEFT if array == K else V_LEFT).start()
        halo_copy(array, head, OWN).start()

    def second(array, head):
        from_left, from_right = (K_RIGHT, K_LEFT) if array == K else (V_RIGHT, V_LEFT)
        x_copy(head, from_left).wait_recv()
        if array == K:
            x_copy(head, K_RELAY).start()
        x_copy(head, from_right).wait_recv()
        if array == V:
            x_copy(head, V_RELAY).start()
        halo_copy(array, head, LEFT).start()
        halo_copy(array, head, RIGHT).start()

    def third(array, head):
        x_copy(head, K_RELAY if array == K else V_RELAY).wait_recv()
        halo_copy(array, head, FAR).start()

    def halo(head):
        for array in (K, V):
            for role in (OWN, LEFT, RIGHT, FAR):
                halo_copy(array, head, role).wait_recv()

    ones = jnp.ones((BLOCK, HEAD_DIM), jnp.bfloat16)

    def attend(head, frame):
        query = qbuf[head, frame]
        allowed_back = reach[frame]
        top = total = None
        for back in range(REACH + 1):
            if back:
                ok = (allowed_back >= back) & (group * FRAMES_HERE + frame >= back)
                bias = jnp.where(ok, jnp.float32(0), jnp.float32(MASKED))
            for part in range(RING_X):
                rows = pl.ds(part * BLOCK, BLOCK)
                scores = lax.dot_general(
                    query, kbuf[head, frame + REACH - back, rows, :], (((1,), (1,)), ((), ())),
                    preferred_element_type=jnp.float32,
                ) * SCALE
                best = jnp.max(scores, axis=1, keepdims=True)
                if back:
                    best = best + bias
                higher = best if top is None else jnp.maximum(top, best)
                weights = jnp.exp2(scores + (bias - higher if back else -higher))
                both = jnp.concatenate([vbuf[head, frame + REACH - back, rows, :], ones], 1)
                product = jnp.dot(weights.astype(jnp.bfloat16), both, preferred_element_type=jnp.float32)
                total = product if top is None else total * jnp.exp2(top - higher) + product
                top = higher
        obuf[head, frame] = (total[:, :HEAD_DIM] / total[:, HEAD_DIM:]).astype(jnp.bfloat16)

    def compute(head, start):
        def body(frame, carry):
            attend(head, frame)
            for step in Y_STEPS:
                o_copy(head, frame, step).start()
            o_own(head, frame).start()
            return carry

        lax.fori_loop(start, start + 2, body, 0)

    def finish(head):
        def waits(frame, carry):
            for step in Y_STEPS:
                o_copy(head, frame, step).wait_recv()
            o_own(head, frame).wait()
            return carry

        lax.fori_loop(0, FRAMES_HERE, waits, 0)
        for frame in range(FRAMES_HERE):
            level = levels[frame] - group * (2 * FRAMES_HERE)
            for owner in range(RING_Y):
                cols = pl.ds((owner * HEADS_HERE + head) * HEAD_DIM, HEAD_DIM)
                pair = gate[pl.ds(2 * frame, 2), cols].astype(jnp.float32)
                low, high = 2 * frame, 2 * frame + 1
                factor = jnp.where(level == low, steps_table[low] * pair[0:1], steps_table[high] * pair[1:2])
                result = lat[frame, :, cols].astype(jnp.float32) - factor * attn[frame, :, cols].astype(jnp.float32)
                result = result.astype(jnp.bfloat16)
                updated[frame, :, cols] = result
                if frame == 0:
                    new[:, cols] = result
                else:
                    next_queue[frame - 1, :, cols] = result

    first(K, 0)
    first(V, 0)
    second(K, 0)
    second(V, 0)
    first(K, 1)
    third(K, 0)
    third(V, 0)
    arrive(Q, 0)
    compute(0, 2)
    first(V, 1)
    second(K, 1)
    halo(0)
    compute(0, 0)
    second(V, 1)
    third(K, 1)
    first(K, 2)
    third(V, 1)
    arrive(Q, 1)
    compute(1, 2)
    second(K, 2)
    first(V, 2)
    halo(1)
    compute(1, 0)
    third(K, 2)
    lat_copy.wait()
    gate_copy.wait()
    finish(0)
    second(V, 2)
    third(V, 2)
    arrive(Q, 2)
    compute(2, 2)
    finish(1)
    halo(2)
    compute(2, 0)
    finish(2)
    frame_copy.start()
    frame_copy.wait_recv()

    is_last = group == GROUPS - 1

    @pl.when(is_last)
    def _():
        copy = pltpu.make_async_copy(fresh, next_queue.at[FRAMES_HERE - 1], in_sem.at[2])
        copy.start()
        copy.wait()

    @pl.when(jnp.logical_not(is_last))
    def _():
        next_queue[FRAMES_HERE - 1] = incoming[...]

    frame_copy.wait_send()
    for array, head in Y_ORDER:
        for step in Y_STEPS:
            y_copy(array, head, step).wait_send()
    for head in range(HEADS_HERE):
        for kind in range(6):
            x_copy(head, kind).wait_send()
        for array in (K, V):
            for role in (OWN, LEFT, RIGHT, FAR):
                halo_copy(array, head, role).wait_send()

        def drain(frame, carry):
            for step in Y_STEPS:
                o_copy(head, frame, step).wait_send()
            return carry

        lax.fori_loop(0, FRAMES_HERE, drain, 0)


def per_device(latents, queries, keys, values, levels, reach, gates, steps_table, fresh):
    shape = (FRAMES_HERE, ROWS, WIDTH)
    bf16 = jnp.bfloat16
    anywhere = pl.BlockSpec(memory_space=pl.ANY)
    scalars = pl.BlockSpec(memory_space=pltpu.SMEM)
    vmem = pl.BlockSpec(memory_space=pltpu.VMEM)
    dma = pltpu.SemaphoreType.DMA
    exchanged = 3 * HEADS_HERE * RING_Y
    window = (HEADS_HERE, FRAMES_HERE + REACH, FRAME_LEN, HEAD_DIM)
    mine = (HEADS_HERE, FRAMES_HERE, BLOCK, HEAD_DIM)
    return pl.pallas_call(
        kernel,
        out_shape=(jax.ShapeDtypeStruct(shape, bf16), jax.ShapeDtypeStruct(shape, bf16)),
        in_specs=[anywhere] * 4 + [scalars, scalars, anywhere, scalars, anywhere],
        out_specs=(vmem, vmem),
        scratch_shapes=[
            pltpu.VMEM(window, bf16),
            pltpu.VMEM(window, bf16),
            pltpu.VMEM(mine, bf16),
            pltpu.VMEM(mine, bf16),
            pltpu.VMEM(shape, bf16),
            pltpu.VMEM(shape, bf16),
            pltpu.VMEM((2 * FRAMES_HERE, WIDTH), bf16),
            pltpu.VMEM((ROWS, WIDTH), bf16),
            pltpu.VMEM((ROWS, WIDTH), bf16),
            dma((exchanged,)),
            dma((exchanged,)),
            dma((3 * HEADS_HERE,)),
            dma((6 * HEADS_HERE,)),
            dma((6 * HEADS_HERE,)),
            dma((8 * HEADS_HERE,)),
            dma((8 * HEADS_HERE,)),
            dma((HEADS_HERE * FRAMES_HERE * RING_Y,)),
            dma((HEADS_HERE * FRAMES_HERE * RING_Y,)),
            dma((HEADS_HERE * FRAMES_HERE,)),
            dma((1,)),
            dma((1,)),
            dma((3,)),
        ],
        compiler_params=pltpu.CompilerParams(
            collective_id=0, has_side_effects=True, vmem_limit_bytes=48 * 1024 * 1024
        ),
        cost_estimate=pl.CostEstimate(
            flops=9_700_000_000, bytes_accessed=8_000_000, transcendentals=9_500_000
        ),
    )(latents, queries, keys, values, levels, reach, gates, steps_table, fresh)


def solution(mesh):
    in_specs = (
        P("frame", "tok", None),
        P("frame", "tok", None),
        P("frame", "tok", None),
        P("frame", "tok", None),
        P("frame"),
        P("frame"),
        P("frame", None),
        P("frame"),
        P("tok", None),
    )
    out_specs = (P("frame", "tok", None), P("frame", "tok", None))
    return jax.shard_map(
        per_device, mesh=mesh, in_specs=in_specs, out_specs=out_specs, check_vma=False
    )
```

```python
import math

import jax
import jax.numpy as jnp
from jax import lax
from jax.experimental import pallas as pl
from jax.experimental.pallas import tpu as pltpu
from jax.sharding import PartitionSpec as P

HEAD_DIM = 128
REACH = 2
FRAMES_HERE = 4
ROWS = 32
RING_Y = 8
RING_X = 4
GROUPS = 16
HEADS_HERE = 3
BLOCK = ROWS * RING_Y
FRAME_LEN = BLOCK * RING_X
WIDTH = RING_Y * HEADS_HERE * HEAD_DIM
PART = RING_Y * HEAD_DIM
SCALE = math.log2(math.e) / math.sqrt(HEAD_DIM)
MASKED = -1e30
MESH = pl.DeviceIdType.MESH
K, V, Q = 0, 1, 2
Y_STEPS = (4, 3, 5, 2, 6, 1, 7)
WHOLE, EARLY, LATE = (0, 4), (0, 2), (2, 2)
TO_RIGHT, TO_LEFT, RELAY_RIGHT, RELAY_LEFT = range(4)
OWN, LEFT, RIGHT, FAR = range(4)
NEAR = (OWN, LEFT, RIGHT)
ALL = (OWN, LEFT, RIGHT, FAR)
SPLIT = ((K, 0), (V, 2))


def pieces(array, head):
    return (LATE, EARLY) if (array, head) in SPLIT else (WHOLE,)


def kernel(
    latents, queries, keys, values, levels, reach, gates, steps_table, fresh,
    updated, next_queue,
    kbuf, vbuf, qbuf, obuf, attn, lat, gate, newest, new, incoming, totals, tops,
    level, window, step_size,
    y_send, y_recv, x_send, x_recv, halo_send, halo_recv,
    o_send, o_recv, f_send, f_recv, in_sem,
):
    group = lax.axis_index("frame")
    place = lax.axis_index("tok")
    y, x = place // RING_X, place % RING_X
    bufs = {K: kbuf, V: vbuf, Q: qbuf}
    sources = {K: keys, V: values, Q: queries}

    def along_y(step):
        return (group, lax.rem(y + step, RING_Y) * RING_X + x)

    def along_x(step):
        return (group, y * RING_X + lax.rem(x + step + RING_X, RING_X))

    def along_frame(step):
        return (lax.rem(group + step + GROUPS, GROUPS), place)

    to_right, to_left = along_x(1), along_x(-1)
    next_group, last_group = along_frame(1), along_frame(-1)

    local = [
        pltpu.make_async_copy(source, target, in_sem.at[index])
        for index, (source, target) in enumerate(
            ((levels, level), (reach, window), (steps_table, step_size), (gates, gate), (latents, lat), (fresh, newest))
        )
    ]

    barrier = pltpu.get_barrier_semaphore()
    peers = [along_y(step) for step in range(1, RING_Y)] + [to_right, to_left, next_group, last_group]
    for peer in peers:
        pl.semaphore_signal(barrier, inc=1, device_id=peer, device_id_type=MESH)
    pl.semaphore_wait(barrier, len(peers))

    def wait(ref, sem):
        pltpu.make_async_copy(ref, ref, sem).wait()

    def columns(owner, head):
        return pl.ds(pl.multiple_of((owner * HEADS_HERE + head) * HEAD_DIM, HEAD_DIM), HEAD_DIM)

    def block_rows(role):
        shift = {OWN: 0, LEFT: 3, RIGHT: 1, FAR: 2}[role]
        return pl.ds(pl.multiple_of(lax.rem(x + shift, RING_X) * BLOCK, BLOCK), BLOCK)

    def unit(array, head, piece):
        return (array * HEADS_HERE + head) * 2 + (piece == EARLY)

    def landing(array, head, piece):
        if array == Q:
            rows = pl.ds(pl.multiple_of(y * ROWS, ROWS), ROWS)
            return qbuf.at[head, pl.ds(*piece), rows, :]
        rows = pl.ds(pl.multiple_of(x * BLOCK + y * ROWS, ROWS), ROWS)
        return bufs[array].at[head, pl.ds(REACH + piece[0], piece[1]), rows, :]

    def y_copy(array, head, piece, step):
        owner = lax.rem(y + step, RING_Y)
        return pltpu.make_async_remote_copy(
            src_ref=sources[array].at[pl.ds(*piece), :, columns(owner, head)],
            dst_ref=landing(array, head, piece),
            send_sem=y_send.at[array * HEADS_HERE + head],
            recv_sem=y_recv.at[unit(array, head, piece)],
            device_id=along_y(step),
            device_id_type=MESH,
        )

    def exchange(array, head):
        for piece in pieces(array, head):
            for step in Y_STEPS:
                y_copy(array, head, piece, step).start()
            pltpu.make_async_copy(
                sources[array].at[pl.ds(*piece), :, columns(y, head)],
                landing(array, head, piece),
                y_recv.at[unit(array, head, piece)],
            ).start()

    def arrive(array, head, piece=WHOLE):
        if array == Q:
            block = qbuf.at[head, pl.ds(*piece)]
        else:
            block = bufs[array].at[head, pl.ds(REACH + piece[0], piece[1]), block_rows(OWN), :]
        wait(block, y_recv.at[unit(array, head, piece)])

    def x_copy(array, head, piece, kind):
        role = {RELAY_RIGHT: LEFT, RELAY_LEFT: RIGHT}.get(kind, OWN)
        first, count = piece
        if kind in (RELAY_RIGHT, RELAY_LEFT):
            count = count // 2
        if kind == RELAY_LEFT:
            first = first + count
        block = bufs[array].at[head, pl.ds(REACH + first, count), block_rows(role), :]
        return pltpu.make_async_remote_copy(
            src_ref=block,
            dst_ref=block,
            send_sem=x_send.at[array * HEADS_HERE + head],
            recv_sem=x_recv.at[unit(array, head, piece) * 4 + kind],
            device_id=to_right if kind in (TO_RIGHT, RELAY_RIGHT) else to_left,
            device_id_type=MESH,
        )

    def halo_index(array, head, far):
        return (array * HEADS_HERE + head) * 2 + far

    def halo_start(array, head, piece, role):
        if piece == EARLY:
            return
        pltpu.make_async_remote_copy(
            src_ref=bufs[array].at[head, pl.ds(FRAMES_HERE, REACH), block_rows(role), :],
            dst_ref=bufs[array].at[head, pl.ds(0, REACH), block_rows(role), :],
            send_sem=halo_send.at[array * HEADS_HERE + head],
            recv_sem=halo_recv.at[halo_index(array, head, role == FAR)],
            device_id=next_group,
            device_id_type=MESH,
        ).start()

    def halo(head, far):
        for array in (K, V):
            rows = pl.ds(0, BLOCK if far else 3 * BLOCK)
            wait(bufs[array].at[head, pl.ds(0, REACH), rows, :], halo_recv.at[halo_index(array, head, far)])

    def first(array, head, piece=WHOLE):
        arrive(array, head, piece)
        x_copy(array, head, piece, TO_RIGHT).start()
        x_copy(array, head, piece, TO_LEFT).start()
        halo_start(array, head, piece, OWN)

    def second(array, head, piece=WHOLE):
        x_copy(array, head, piece, TO_RIGHT).wait_recv()
        x_copy(array, head, piece, RELAY_RIGHT).start()
        x_copy(array, head, piece, TO_LEFT).wait_recv()
        x_copy(array, head, piece, RELAY_LEFT).start()
        halo_start(array, head, piece, LEFT)
        halo_start(array, head, piece, RIGHT)

    def third(array, head, piece=WHOLE):
        x_copy(array, head, piece, RELAY_RIGHT).wait_recv()
        x_copy(array, head, piece, RELAY_LEFT).wait_recv()
        halo_start(array, head, piece, FAR)

    ones = jnp.ones((BLOCK, HEAD_DIM), jnp.bfloat16)

    def attend(head, frame, roles, begin, end):
        query = qbuf[head, frame]
        allowed_back = window[frame]
        if begin:
            top = total = None
        else:
            top, total = tops[frame][:, :1], totals[frame]
        for back in range(REACH + 1):
            ok = (allowed_back >= back) & (group * FRAMES_HERE + frame >= back)
            bias = jnp.where(ok, jnp.float32(0), jnp.float32(MASKED))
            for role in roles:
                rows = block_rows(role)
                scores = lax.dot_general(
                    query, kbuf[head, frame + REACH - back, rows, :], (((1,), (1,)), ((), ())),
                    preferred_element_type=jnp.float32,
                ) * SCALE
                best = jnp.max(scores, axis=1, keepdims=True)
                if back:
                    best = best + bias
                higher = best if top is None else jnp.maximum(top, best)
                weights = jnp.exp2(scores + (bias - higher if back else -higher))
                both = jnp.concatenate([vbuf[head, frame + REACH - back, rows, :], ones], 1)
                product = jnp.dot(weights.astype(jnp.bfloat16), both, preferred_element_type=jnp.float32)
                total = product if top is None else total * jnp.exp2(top - higher) + product
                top = higher
        if end:
            obuf[head, frame] = (total[:, :HEAD_DIM] / total[:, HEAD_DIM:]).astype(jnp.bfloat16)
        else:
            tops[frame] = jnp.broadcast_to(top, (BLOCK, HEAD_DIM))
            totals[frame] = total

    def give_back(head, frame):
        for step in Y_STEPS:
            rows = pl.ds(pl.multiple_of(lax.rem(y + step, RING_Y) * ROWS, ROWS), ROWS)
            pltpu.make_async_remote_copy(
                src_ref=obuf.at[head, frame, rows, :],
                dst_ref=attn.at[frame, :, columns(y, head)],
                send_sem=o_send.at[head],
                recv_sem=o_recv.at[head * FRAMES_HERE + frame],
                device_id=along_y(step),
                device_id_type=MESH,
            ).start()
        rows = pl.ds(pl.multiple_of(y * ROWS, ROWS), ROWS)
        pltpu.make_async_copy(
            obuf.at[head, frame, rows, :],
            attn.at[frame, :, columns(y, head)],
            o_recv.at[head * FRAMES_HERE + frame],
        ).start()

    def compute(head, start, count, roles=ALL, begin=True, end=True):
        def body(frame, carry):
            attend(head, frame, roles, begin, end)
            if end:
                give_back(head, frame)
            return carry

        lax.fori_loop(start, start + count, body, 0)

    def frame_copy(head):
        return pltpu.make_async_remote_copy(
            src_ref=new.at[head],
            dst_ref=incoming.at[head],
            send_sem=f_send.at[head],
            recv_sem=f_recv.at[head],
            device_id=last_group,
            device_id_type=MESH,
        )

    def finish(head, start, count):
        for frame in range(start, start + count):
            wait(attn.at[frame, :, pl.ds(0, PART)], o_recv.at[head * FRAMES_HERE + frame])
            low, high = 2 * frame, 2 * frame + 1
            is_low = level[frame] == group * (2 * FRAMES_HERE) + low
            for owner in range(RING_Y):
                cols = pl.ds((owner * HEADS_HERE + head) * HEAD_DIM, HEAD_DIM)
                pair = gate[:, cols].astype(jnp.float32)
                factor = jnp.where(is_low, step_size[low] * pair[low:high], step_size[high] * pair[high:high + 1])
                result = lat[frame, :, cols].astype(jnp.float32) - factor * attn[frame, :, cols].astype(jnp.float32)
                result = result.astype(jnp.bfloat16)
                updated[frame, :, cols] = result
                if frame == 0:
                    new[head, :, pl.ds(owner * HEAD_DIM, HEAD_DIM)] = result
                else:
                    next_queue[frame - 1, :, cols] = result
            if frame == 0:
                frame_copy(head).start()

    is_last = group == GROUPS - 1

    def enter(head):
        frame_copy(head).wait_recv()
        for owner in range(RING_Y):
            cols = pl.ds((owner * HEADS_HERE + head) * HEAD_DIM, HEAD_DIM)
            came = incoming[head, :, pl.ds(owner * HEAD_DIM, HEAD_DIM)]
            next_queue[FRAMES_HERE - 1, :, cols] = jnp.where(is_last, newest[:, cols], came)

    def prepare():
        for copy in local:
            copy.start()

    def prepared():
        for copy in local:
            copy.wait()

    exchange(K, 0)
    exchange(V, 0)
    exchange(K, 1)
    exchange(Q, 0)
    exchange(V, 1)
    exchange(K, 2)
    exchange(Q, 1)
    exchange(V, 2)
    exchange(Q, 2)
    prepare()
    first(K, 0, LATE)
    first(K, 0, EARLY)
    first(V, 0)
    second(K, 0, LATE)
    second(K, 0, EARLY)
    prepared()
    second(V, 0)
    first(K, 1)
    third(K, 0, LATE)
    third(K, 0, EARLY)
    third(V, 0)
    arrive(Q, 0)
    compute(0, 2, 2)
    first(V, 1)
    second(K, 1)
    halo(0, False)
    halo(0, True)
    compute(0, 0, 2)
    second(V, 1)
    third(K, 1)
    first(K, 2)
    third(V, 1)
    arrive(Q, 1)
    compute(1, 2, 2)
    second(K, 2)
    first(V, 2, LATE)
    first(V, 2, EARLY)
    halo(1, False)
    halo(1, True)
    compute(1, 0, 2)
    third(K, 2)
    second(V, 2, LATE)
    second(V, 2, EARLY)
    arrive(Q, 2)
    third(V, 2, LATE)
    third(V, 2, EARLY)
    compute(2, 2, 2)
    halo(2, False)
    halo(2, True)
    compute(2, 0, 2)
    finish(0, 0, 4)
    finish(1, 0, 4)
    finish(2, 0, 1)
    finish(2, 1, 3)
    enter(0)
    enter(1)
    enter(2)

    away = BLOCK - ROWS
    for head in range(HEADS_HERE):
        frame_copy(head).wait_send()
        for array in (K, V, Q):
            wait(qbuf.at[head, :, pl.ds(0, away), :], y_send.at[array * HEADS_HERE + head])
        for array in (K, V):
            index = array * HEADS_HERE + head
            wait(bufs[array].at[head, pl.ds(0, FRAMES_HERE), pl.ds(0, 3 * BLOCK), :], x_send.at[index])
            wait(bufs[array].at[head, pl.ds(0, REACH)], halo_send.at[index])
        wait(obuf.at[head, :, pl.ds(0, away), :], o_send.at[head])


def per_device(latents, queries, keys, values, levels, reach, gates, steps_table, fresh):
    shape = (FRAMES_HERE, ROWS, WIDTH)
    bf16 = jnp.bfloat16
    hbm = pl.BlockSpec(memory_space=pltpu.HBM)
    vmem = pl.BlockSpec(memory_space=pltpu.VMEM)
    dma = pltpu.SemaphoreType.DMA
    span = (HEADS_HERE, FRAMES_HERE + REACH, FRAME_LEN, HEAD_DIM)
    mine = (HEADS_HERE, FRAMES_HERE, BLOCK, HEAD_DIM)
    return pl.pallas_call(
        kernel,
        out_shape=(jax.ShapeDtypeStruct(shape, bf16), jax.ShapeDtypeStruct(shape, bf16)),
        in_specs=[hbm] * 9,
        out_specs=(vmem, vmem),
        scratch_shapes=[
            pltpu.VMEM(span, bf16),
            pltpu.VMEM(span, bf16),
            pltpu.VMEM(mine, bf16),
            pltpu.VMEM(mine, bf16),
            pltpu.VMEM(shape, bf16),
            pltpu.VMEM(shape, bf16),
            pltpu.VMEM((2 * FRAMES_HERE, WIDTH), bf16),
            pltpu.VMEM((ROWS, WIDTH), bf16),
            pltpu.VMEM((HEADS_HERE, ROWS, PART), bf16),
            pltpu.VMEM((HEADS_HERE, ROWS, PART), bf16),
            pltpu.VMEM((FRAMES_HERE, BLOCK, 2 * HEAD_DIM), jnp.float32),
            pltpu.VMEM((FRAMES_HERE, BLOCK, HEAD_DIM), jnp.float32),
            pltpu.SMEM((FRAMES_HERE,), jnp.int32),
            pltpu.SMEM((FRAMES_HERE,), jnp.int32),
            pltpu.SMEM((2 * FRAMES_HERE,), jnp.float32),
            dma((3 * HEADS_HERE,)),
            dma((6 * HEADS_HERE,)),
            dma((2 * HEADS_HERE,)),
            dma((16 * HEADS_HERE,)),
            dma((2 * HEADS_HERE,)),
            dma((4 * HEADS_HERE,)),
            dma((HEADS_HERE,)),
            dma((HEADS_HERE * FRAMES_HERE,)),
            dma((HEADS_HERE,)),
            dma((HEADS_HERE,)),
            dma((6,)),
        ],
        compiler_params=pltpu.CompilerParams(
            collective_id=0, has_side_effects=True, vmem_limit_bytes=62 * 1024 * 1024
        ),
        cost_estimate=pl.CostEstimate(
            flops=9_700_000_000, bytes_accessed=8_000_000, transcendentals=9_500_000
        ),
    )(latents, queries, keys, values, levels, reach, gates, steps_table, fresh)


def solution(mesh):
    in_specs = (
        P("frame", "tok", None),
        P("frame", "tok", None),
        P("frame", "tok", None),
        P("frame", "tok", None),
        P("frame"),
        P("frame"),
        P("frame", None),
        P("frame"),
        P("tok", None),
    )
    out_specs = (P("frame", "tok", None), P("frame", "tok", None))
    return jax.shard_map(
        per_device, mesh=mesh, in_specs=in_specs, out_specs=out_specs, check_vma=False
    )
```

```python
import math

import jax
import jax.numpy as jnp
from jax import lax
from jax.experimental import pallas as pl
from jax.experimental.pallas import tpu as pltpu
from jax.sharding import PartitionSpec as P

HEAD_DIM = 128
REACH = 2
FRAMES_HERE = 4
ROWS = 32
RING_Y = 8
RING_X = 4
GROUPS = 16
HEADS_HERE = 3
BLOCK = ROWS * RING_Y
FRAME_LEN = BLOCK * RING_X
WIDTH = RING_Y * HEADS_HERE * HEAD_DIM
PART = RING_Y * HEAD_DIM
SCALE = math.log2(math.e) / math.sqrt(HEAD_DIM)
MASKED = -1e30
MESH = pl.DeviceIdType.MESH
K, V, Q = 0, 1, 2
Y_STEPS = (4, 3, 5, 2, 6, 1, 7)
WHOLE, EARLY, LATE = (0, 4), (0, 2), (2, 2)
TO_RIGHT, TO_LEFT, RELAY_RIGHT, RELAY_LEFT = range(4)
OWN, LEFT, RIGHT, FAR = range(4)
NEAR = (OWN, LEFT, RIGHT)
ALL = (OWN, LEFT, RIGHT, FAR)
SPLIT = tuple((a, h) for a in (K, V) for h in range(HEADS_HERE))


def pieces(array, head):
    return (LATE, EARLY) if (array, head) in SPLIT else (WHOLE,)


def kernel(
    latents, queries, keys, values, levels, reach, gates, steps_table, fresh,
    updated, next_queue,
    kbuf, vbuf, qbuf, obuf, attn, lat, gate, newest, new, incoming, totals, tops,
    level, window, step_size,
    y_send, y_recv, x_send, x_recv, halo_send, halo_recv,
    o_send, o_recv, f_send, f_recv, in_sem,
):
    group = lax.axis_index("frame")
    place = lax.axis_index("tok")
    y, x = place // RING_X, place % RING_X
    bufs = {K: kbuf, V: vbuf, Q: qbuf}
    sources = {K: keys, V: values, Q: queries}

    def along_y(step):
        return (group, lax.rem(y + step, RING_Y) * RING_X + x)

    def along_x(step):
        return (group, y * RING_X + lax.rem(x + step + RING_X, RING_X))

    def along_frame(step):
        return (lax.rem(group + step + GROUPS, GROUPS), place)

    to_right, to_left = along_x(1), along_x(-1)
    next_group, last_group = along_frame(1), along_frame(-1)

    local = [
        pltpu.make_async_copy(source, target, in_sem.at[index])
        for index, (source, target) in enumerate(
            ((levels, level), (reach, window), (steps_table, step_size), (gates, gate), (latents, lat), (fresh, newest))
        )
    ]

    barrier = pltpu.get_barrier_semaphore()
    peers = [along_y(step) for step in range(1, RING_Y)] + [to_right, to_left, next_group, last_group]
    for peer in peers:
        pl.semaphore_signal(barrier, inc=1, device_id=peer, device_id_type=MESH)
    pl.semaphore_wait(barrier, len(peers))

    def wait(ref, sem):
        pltpu.make_async_copy(ref, ref, sem).wait()

    def columns(owner, head):
        return pl.ds(pl.multiple_of((owner * HEADS_HERE + head) * HEAD_DIM, HEAD_DIM), HEAD_DIM)

    def block_rows(role):
        shift = {OWN: 0, LEFT: 3, RIGHT: 1, FAR: 2}[role]
        return pl.ds(pl.multiple_of(lax.rem(x + shift, RING_X) * BLOCK, BLOCK), BLOCK)

    def unit(array, head, piece):
        return (array * HEADS_HERE + head) * 2 + (piece == EARLY)

    def landing(array, head, piece):
        if array == Q:
            rows = pl.ds(pl.multiple_of(y * ROWS, ROWS), ROWS)
            return qbuf.at[head, pl.ds(*piece), rows, :]
        rows = pl.ds(pl.multiple_of(x * BLOCK + y * ROWS, ROWS), ROWS)
        return bufs[array].at[head, pl.ds(REACH + piece[0], piece[1]), rows, :]

    def y_copy(array, head, piece, step):
        owner = lax.rem(y + step, RING_Y)
        return pltpu.make_async_remote_copy(
            src_ref=sources[array].at[pl.ds(*piece), :, columns(owner, head)],
            dst_ref=landing(array, head, piece),
            send_sem=y_send.at[array * HEADS_HERE + head],
            recv_sem=y_recv.at[unit(array, head, piece)],
            device_id=along_y(step),
            device_id_type=MESH,
        )

    def exchange(array, head):
        for piece in pieces(array, head):
            for step in Y_STEPS:
                y_copy(array, head, piece, step).start()
            pltpu.make_async_copy(
                sources[array].at[pl.ds(*piece), :, columns(y, head)],
                landing(array, head, piece),
                y_recv.at[unit(array, head, piece)],
            ).start()

    def arrive(array, head, piece=WHOLE):
        if array == Q:
            block = qbuf.at[head, pl.ds(*piece)]
        else:
            block = bufs[array].at[head, pl.ds(REACH + piece[0], piece[1]), block_rows(OWN), :]
        wait(block, y_recv.at[unit(array, head, piece)])

    def x_copy(array, head, piece, kind):
        role = {RELAY_RIGHT: LEFT, RELAY_LEFT: RIGHT}.get(kind, OWN)
        first, count = piece
        if kind in (RELAY_RIGHT, RELAY_LEFT):
            count = count // 2
        if kind == RELAY_LEFT:
            first = first + count
        block = bufs[array].at[head, pl.ds(REACH + first, count), block_rows(role), :]
        return pltpu.make_async_remote_copy(
            src_ref=block,
            dst_ref=block,
            send_sem=x_send.at[array * HEADS_HERE + head],
            recv_sem=x_recv.at[unit(array, head, piece) * 4 + kind],
            device_id=to_right if kind in (TO_RIGHT, RELAY_RIGHT) else to_left,
            device_id_type=MESH,
        )

    def halo_index(array, head, far):
        return (array * HEADS_HERE + head) * 2 + far

    def halo_start(array, head, piece, role):
        if piece == EARLY:
            return
        pltpu.make_async_remote_copy(
            src_ref=bufs[array].at[head, pl.ds(FRAMES_HERE, REACH), block_rows(role), :],
            dst_ref=bufs[array].at[head, pl.ds(0, REACH), block_rows(role), :],
            send_sem=halo_send.at[array * HEADS_HERE + head],
            recv_sem=halo_recv.at[halo_index(array, head, role == FAR)],
            device_id=next_group,
            device_id_type=MESH,
        ).start()

    def halo(head, far):
        for array in (K, V):
            rows = pl.ds(0, BLOCK if far else 3 * BLOCK)
            wait(bufs[array].at[head, pl.ds(0, REACH), rows, :], halo_recv.at[halo_index(array, head, far)])

    def first(array, head, piece=WHOLE):
        arrive(array, head, piece)
        x_copy(array, head, piece, TO_RIGHT).start()
        x_copy(array, head, piece, TO_LEFT).start()
        halo_start(array, head, piece, OWN)

    def second(array, head, piece=WHOLE):
        x_copy(array, head, piece, TO_RIGHT).wait_recv()
        x_copy(array, head, piece, RELAY_RIGHT).start()
        x_copy(array, head, piece, TO_LEFT).wait_recv()
        x_copy(array, head, piece, RELAY_LEFT).start()
        halo_start(array, head, piece, LEFT)
        halo_start(array, head, piece, RIGHT)

    def third(array, head, piece=WHOLE):
        x_copy(array, head, piece, RELAY_RIGHT).wait_recv()
        x_copy(array, head, piece, RELAY_LEFT).wait_recv()
        halo_start(array, head, piece, FAR)

    ones = jnp.ones((BLOCK, HEAD_DIM), jnp.bfloat16)

    def attend(head, frame, roles, begin, end):
        query = qbuf[head, frame]
        allowed_back = window[frame]
        if begin:
            top = total = None
        else:
            top, total = tops[frame][:, :1], totals[frame]
        for back in range(REACH + 1):
            ok = (allowed_back >= back) & (group * FRAMES_HERE + frame >= back)
            bias = jnp.where(ok, jnp.float32(0), jnp.float32(MASKED))
            for role in roles:
                rows = block_rows(role)
                scores = lax.dot_general(
                    query, kbuf[head, frame + REACH - back, rows, :], (((1,), (1,)), ((), ())),
                    preferred_element_type=jnp.float32,
                ) * SCALE
                best = jnp.max(scores, axis=1, keepdims=True)
                if back:
                    best = best + bias
                higher = best if top is None else jnp.maximum(top, best)
                weights = jnp.exp2(scores + (bias - higher if back else -higher))
                both = jnp.concatenate([vbuf[head, frame + REACH - back, rows, :], ones], 1)
                product = jnp.dot(weights.astype(jnp.bfloat16), both, preferred_element_type=jnp.float32)
                total = product if top is None else total * jnp.exp2(top - higher) + product
                top = higher
        if end:
            obuf[head, frame] = (total[:, :HEAD_DIM] / total[:, HEAD_DIM:]).astype(jnp.bfloat16)
        else:
            tops[frame] = jnp.broadcast_to(top, (BLOCK, HEAD_DIM))
            totals[frame] = total

    def give_back(head, frame):
        for step in Y_STEPS:
            rows = pl.ds(pl.multiple_of(lax.rem(y + step, RING_Y) * ROWS, ROWS), ROWS)
            pltpu.make_async_remote_copy(
                src_ref=obuf.at[head, frame, rows, :],
                dst_ref=attn.at[frame, :, columns(y, head)],
                send_sem=o_send.at[head],
                recv_sem=o_recv.at[head * FRAMES_HERE + frame],
                device_id=along_y(step),
                device_id_type=MESH,
            ).start()
        rows = pl.ds(pl.multiple_of(y * ROWS, ROWS), ROWS)
        pltpu.make_async_copy(
            obuf.at[head, frame, rows, :],
            attn.at[frame, :, columns(y, head)],
            o_recv.at[head * FRAMES_HERE + frame],
        ).start()

    def compute(head, start, count, roles=ALL, begin=True, end=True):
        def body(frame, carry):
            attend(head, frame, roles, begin, end)
            if end:
                give_back(head, frame)
            return carry

        lax.fori_loop(start, start + count, body, 0)

    def frame_copy(head):
        return pltpu.make_async_remote_copy(
            src_ref=new.at[head],
            dst_ref=incoming.at[head],
            send_sem=f_send.at[head],
            recv_sem=f_recv.at[head],
            device_id=last_group,
            device_id_type=MESH,
        )

    def finish(head, start, count):
        for frame in range(start, start + count):
            wait(attn.at[frame, :, pl.ds(0, PART)], o_recv.at[head * FRAMES_HERE + frame])
            low, high = 2 * frame, 2 * frame + 1
            is_low = level[frame] == group * (2 * FRAMES_HERE) + low
            for owner in range(RING_Y):
                cols = pl.ds((owner * HEADS_HERE + head) * HEAD_DIM, HEAD_DIM)
                pair = gate[:, cols].astype(jnp.float32)
                factor = jnp.where(is_low, step_size[low] * pair[low:high], step_size[high] * pair[high:high + 1])
                result = lat[frame, :, cols].astype(jnp.float32) - factor * attn[frame, :, cols].astype(jnp.float32)
                result = result.astype(jnp.bfloat16)
                updated[frame, :, cols] = result
                if frame == 0:
                    new[head, :, pl.ds(owner * HEAD_DIM, HEAD_DIM)] = result
                else:
                    next_queue[frame - 1, :, cols] = result
            if frame == 0:
                frame_copy(head).start()

    is_last = group == GROUPS - 1

    def enter(head):
        frame_copy(head).wait_recv()
        for owner in range(RING_Y):
            cols = pl.ds((owner * HEADS_HERE + head) * HEAD_DIM, HEAD_DIM)
            came = incoming[head, :, pl.ds(owner * HEAD_DIM, HEAD_DIM)]
            next_queue[FRAMES_HERE - 1, :, cols] = jnp.where(is_last, newest[:, cols], came)

    def prepare():
        for copy in local:
            copy.start()

    def prepared():
        for copy in local:
            copy.wait()

    exchange(K, 0)
    exchange(V, 0)
    exchange(K, 1)
    exchange(Q, 0)
    exchange(V, 1)
    exchange(K, 2)
    exchange(Q, 1)
    exchange(V, 2)
    exchange(Q, 2)
    prepare()
    first(K, 0, LATE)
    first(K, 0, EARLY)
    first(V, 0, LATE)
    first(V, 0, EARLY)
    second(K, 0, LATE)
    second(K, 0, EARLY)
    prepared()
    second(V, 0, LATE)
    second(V, 0, EARLY)
    first(K, 1, LATE)
    first(K, 1, EARLY)
    third(K, 0, LATE)
    third(K, 0, EARLY)
    third(V, 0, LATE)
    third(V, 0, EARLY)
    arrive(Q, 0)
    compute(0, 2, 2)
    first(V, 1, LATE)
    first(V, 1, EARLY)
    second(K, 1, LATE)
    second(K, 1, EARLY)
    halo(0, False)
    halo(0, True)
    compute(0, 0, 2)
    second(V, 1, LATE)
    second(V, 1, EARLY)
    third(K, 1, LATE)
    third(K, 1, EARLY)
    first(K, 2, LATE)
    first(K, 2, EARLY)
    third(V, 1, LATE)
    third(V, 1, EARLY)
    arrive(Q, 1)
    compute(1, 2, 2)
    second(K, 2, LATE)
    second(K, 2, EARLY)
    first(V, 2, LATE)
    first(V, 2, EARLY)
    halo(1, False)
    halo(1, True)
    compute(1, 0, 2)
    third(K, 2, LATE)
    third(K, 2, EARLY)
    second(V, 2, LATE)
    second(V, 2, EARLY)
    arrive(Q, 2)
    third(V, 2, LATE)
    third(V, 2, EARLY)
    compute(2, 2, 1)
    halo(2, False)
    halo(2, True)
    compute(2, 0, 2)
    compute(2, 3, 1)
    finish(0, 0, 4)
    finish(1, 0, 4)
    finish(2, 0, 1)
    enter(0)
    enter(1)
    finish(2, 1, 3)
    enter(2)

    away = BLOCK - ROWS
    for head in range(HEADS_HERE):
        frame_copy(head).wait_send()
        for array in (K, V, Q):
            wait(qbuf.at[head, :, pl.ds(0, away), :], y_send.at[array * HEADS_HERE + head])
        for array in (K, V):
            index = array * HEADS_HERE + head
            wait(bufs[array].at[head, pl.ds(0, FRAMES_HERE), pl.ds(0, 3 * BLOCK), :], x_send.at[index])
            wait(bufs[array].at[head, pl.ds(0, REACH)], halo_send.at[index])
        wait(obuf.at[head, :, pl.ds(0, away), :], o_send.at[head])


def per_device(latents, queries, keys, values, levels, reach, gates, steps_table, fresh):
    shape = (FRAMES_HERE, ROWS, WIDTH)
    bf16 = jnp.bfloat16
    hbm = pl.BlockSpec(memory_space=pltpu.HBM)
    vmem = pl.BlockSpec(memory_space=pltpu.VMEM)
    dma = pltpu.SemaphoreType.DMA
    span = (HEADS_HERE, FRAMES_HERE + REACH, FRAME_LEN, HEAD_DIM)
    mine = (HEADS_HERE, FRAMES_HERE, BLOCK, HEAD_DIM)
    return pl.pallas_call(
        kernel,
        out_shape=(jax.ShapeDtypeStruct(shape, bf16), jax.ShapeDtypeStruct(shape, bf16)),
        in_specs=[hbm] * 9,
        out_specs=(vmem, vmem),
        scratch_shapes=[
            pltpu.VMEM(span, bf16),
            pltpu.VMEM(span, bf16),
            pltpu.VMEM(mine, bf16),
            pltpu.VMEM(mine, bf16),
            pltpu.VMEM(shape, bf16),
            pltpu.VMEM(shape, bf16),
            pltpu.VMEM((2 * FRAMES_HERE, WIDTH), bf16),
            pltpu.VMEM((ROWS, WIDTH), bf16),
            pltpu.VMEM((HEADS_HERE, ROWS, PART), bf16),
            pltpu.VMEM((HEADS_HERE, ROWS, PART), bf16),
            pltpu.VMEM((FRAMES_HERE, BLOCK, 2 * HEAD_DIM), jnp.float32),
            pltpu.VMEM((FRAMES_HERE, BLOCK, HEAD_DIM), jnp.float32),
            pltpu.SMEM((FRAMES_HERE,), jnp.int32),
            pltpu.SMEM((FRAMES_HERE,), jnp.int32),
            pltpu.SMEM((2 * FRAMES_HERE,), jnp.float32),
            dma((3 * HEADS_HERE,)),
            dma((6 * HEADS_HERE,)),
            dma((2 * HEADS_HERE,)),
            dma((16 * HEADS_HERE,)),
            dma((2 * HEADS_HERE,)),
            dma((4 * HEADS_HERE,)),
            dma((HEADS_HERE,)),
            dma((HEADS_HERE * FRAMES_HERE,)),
            dma((HEADS_HERE,)),
            dma((HEADS_HERE,)),
            dma((6,)),
        ],
        compiler_params=pltpu.CompilerParams(
            collective_id=0, has_side_effects=True, vmem_limit_bytes=62 * 1024 * 1024
        ),
        cost_estimate=pl.CostEstimate(
            flops=9_700_000_000, bytes_accessed=8_000_000, transcendentals=9_500_000
        ),
    )(latents, queries, keys, values, levels, reach, gates, steps_table, fresh)


def solution(mesh):
    in_specs = (
        P("frame", "tok", None),
        P("frame", "tok", None),
        P("frame", "tok", None),
        P("frame", "tok", None),
        P("frame"),
        P("frame"),
        P("frame", None),
        P("frame"),
        P("tok", None),
    )
    out_specs = (P("frame", "tok", None), P("frame", "tok", None))
    return jax.shard_map(
        per_device, mesh=mesh, in_specs=in_specs, out_specs=out_specs, check_vma=False
    )
```

```python
import math

import jax
import jax.numpy as jnp
from jax import lax
from jax.experimental import pallas as pl
from jax.experimental.pallas import tpu as pltpu
from jax.sharding import PartitionSpec as P

HEAD_DIM = 128
REACH = 2
FRAMES_HERE = 4
ROWS = 32
RING_Y = 8
RING_X = 4
GROUPS = 16
HEADS_HERE = 3
BLOCK = ROWS * RING_Y
FRAME_LEN = BLOCK * RING_X
WIDTH = RING_Y * HEADS_HERE * HEAD_DIM
PART = RING_Y * HEAD_DIM
SCALE = math.log2(math.e) / math.sqrt(HEAD_DIM)
MASKED = -1e30
MESH = pl.DeviceIdType.MESH
K, V, Q = 0, 1, 2
Y_STEPS = (4, 3, 5, 2, 6, 1, 7)
WHOLE, EARLY, LATE = (0, 4), (0, 2), (2, 2)
TO_RIGHT, TO_LEFT, RELAY_RIGHT, RELAY_LEFT = range(4)
OWN, LEFT, RIGHT, FAR = range(4)
NEAR = (OWN, LEFT, RIGHT)
ALL = (OWN, LEFT, RIGHT, FAR)
SPLIT = tuple((a, h) for a in (K, V) for h in range(HEADS_HERE))


def pieces(array, head):
    return (LATE, EARLY) if (array, head) in SPLIT else (WHOLE,)


def kernel(
    latents, queries, keys, values, levels, reach, gates, steps_table,
    attended, next_queue, factors,
    kbuf, vbuf, qbuf, obuf, attn, lat, gate, new, incoming, totals, tops,
    level, window, step_size,
    y_send, y_recv, x_send, x_recv, halo_send, halo_recv,
    o_send, o_recv, f_send, f_recv, in_sem,
):
    group = lax.axis_index("frame")
    place = lax.axis_index("tok")
    y, x = place // RING_X, place % RING_X
    bufs = {K: kbuf, V: vbuf, Q: qbuf}
    sources = {K: keys, V: values, Q: queries}

    def along_y(step):
        return (group, lax.rem(y + step, RING_Y) * RING_X + x)

    def along_x(step):
        return (group, y * RING_X + lax.rem(x + step + RING_X, RING_X))

    def along_frame(step):
        return (lax.rem(group + step + GROUPS, GROUPS), place)

    to_right, to_left = along_x(1), along_x(-1)
    next_group, last_group = along_frame(1), along_frame(-1)

    local = [
        pltpu.make_async_copy(source, target, in_sem.at[index])
        for index, (source, target) in enumerate(
            ((levels, level), (reach, window), (steps_table, step_size), (gates, gate), (latents, lat))
        )
    ]

    barrier = pltpu.get_barrier_semaphore()
    peers = [along_y(step) for step in range(1, RING_Y)] + [to_right, to_left, next_group, last_group]
    for peer in peers:
        pl.semaphore_signal(barrier, inc=1, device_id=peer, device_id_type=MESH)
    pl.semaphore_wait(barrier, len(peers))

    def wait(ref, sem):
        pltpu.make_async_copy(ref, ref, sem).wait()

    def columns(owner, head):
        return pl.ds(pl.multiple_of((owner * HEADS_HERE + head) * HEAD_DIM, HEAD_DIM), HEAD_DIM)

    def block_rows(role):
        shift = {OWN: 0, LEFT: 3, RIGHT: 1, FAR: 2}[role]
        return pl.ds(pl.multiple_of(lax.rem(x + shift, RING_X) * BLOCK, BLOCK), BLOCK)

    def unit(array, head, piece):
        return (array * HEADS_HERE + head) * 2 + (piece == EARLY)

    def landing(array, head, piece):
        if array == Q:
            rows = pl.ds(pl.multiple_of(y * ROWS, ROWS), ROWS)
            return qbuf.at[head, pl.ds(*piece), rows, :]
        rows = pl.ds(pl.multiple_of(x * BLOCK + y * ROWS, ROWS), ROWS)
        return bufs[array].at[head, pl.ds(REACH + piece[0], piece[1]), rows, :]

    def y_copy(array, head, piece, step):
        owner = lax.rem(y + step, RING_Y)
        return pltpu.make_async_remote_copy(
            src_ref=sources[array].at[pl.ds(*piece), :, columns(owner, head)],
            dst_ref=landing(array, head, piece),
            send_sem=y_send.at[array * HEADS_HERE + head],
            recv_sem=y_recv.at[unit(array, head, piece)],
            device_id=along_y(step),
            device_id_type=MESH,
        )

    def exchange(array, head):
        for piece in pieces(array, head):
            for step in Y_STEPS:
                y_copy(array, head, piece, step).start()
            pltpu.make_async_copy(
                sources[array].at[pl.ds(*piece), :, columns(y, head)],
                landing(array, head, piece),
                y_recv.at[unit(array, head, piece)],
            ).start()

    def arrive(array, head, piece=WHOLE):
        if array == Q:
            block = qbuf.at[head, pl.ds(*piece)]
        else:
            block = bufs[array].at[head, pl.ds(REACH + piece[0], piece[1]), block_rows(OWN), :]
        wait(block, y_recv.at[unit(array, head, piece)])

    def x_copy(array, head, piece, kind):
        role = {RELAY_RIGHT: LEFT, RELAY_LEFT: RIGHT}.get(kind, OWN)
        first, count = piece
        if kind in (RELAY_RIGHT, RELAY_LEFT):
            count = count // 2
        if kind == RELAY_LEFT:
            first = first + count
        block = bufs[array].at[head, pl.ds(REACH + first, count), block_rows(role), :]
        return pltpu.make_async_remote_copy(
            src_ref=block,
            dst_ref=block,
            send_sem=x_send.at[array * HEADS_HERE + head],
            recv_sem=x_recv.at[unit(array, head, piece) * 4 + kind],
            device_id=to_right if kind in (TO_RIGHT, RELAY_RIGHT) else to_left,
            device_id_type=MESH,
        )

    def halo_index(array, head, far):
        return (array * HEADS_HERE + head) * 2 + far

    def halo_start(array, head, piece, role):
        if piece == EARLY:
            return
        pltpu.make_async_remote_copy(
            src_ref=bufs[array].at[head, pl.ds(FRAMES_HERE, REACH), block_rows(role), :],
            dst_ref=bufs[array].at[head, pl.ds(0, REACH), block_rows(role), :],
            send_sem=halo_send.at[array * HEADS_HERE + head],
            recv_sem=halo_recv.at[halo_index(array, head, role == FAR)],
            device_id=next_group,
            device_id_type=MESH,
        ).start()

    def halo(head, far):
        for array in (K, V):
            rows = pl.ds(0, BLOCK if far else 3 * BLOCK)
            wait(bufs[array].at[head, pl.ds(0, REACH), rows, :], halo_recv.at[halo_index(array, head, far)])

    def first(array, head, piece=WHOLE):
        arrive(array, head, piece)
        x_copy(array, head, piece, TO_RIGHT).start()
        x_copy(array, head, piece, TO_LEFT).start()
        halo_start(array, head, piece, OWN)

    def second(array, head, piece=WHOLE):
        x_copy(array, head, piece, TO_RIGHT).wait_recv()
        x_copy(array, head, piece, RELAY_RIGHT).start()
        x_copy(array, head, piece, TO_LEFT).wait_recv()
        x_copy(array, head, piece, RELAY_LEFT).start()
        halo_start(array, head, piece, LEFT)
        halo_start(array, head, piece, RIGHT)

    def third(array, head, piece=WHOLE):
        x_copy(array, head, piece, RELAY_RIGHT).wait_recv()
        x_copy(array, head, piece, RELAY_LEFT).wait_recv()
        halo_start(array, head, piece, FAR)

    ones = jnp.ones((BLOCK, HEAD_DIM), jnp.bfloat16)

    def attend(head, frame, roles, begin, end):
        query = qbuf[head, frame]
        allowed_back = window[frame]
        if begin:
            top = total = None
        else:
            top, total = tops[frame][:, :1], totals[frame]
        for back in range(REACH + 1):
            ok = (allowed_back >= back) & (group * FRAMES_HERE + frame >= back)
            bias = jnp.where(ok, jnp.float32(0), jnp.float32(MASKED))
            for role in roles:
                rows = block_rows(role)
                scores = lax.dot_general(
                    query, kbuf[head, frame + REACH - back, rows, :], (((1,), (1,)), ((), ())),
                    preferred_element_type=jnp.float32,
                ) * SCALE
                best = jnp.max(scores, axis=1, keepdims=True)
                if back:
                    best = best + bias
                higher = best if top is None else jnp.maximum(top, best)
                weights = jnp.exp2(scores + (bias - higher if back else -higher))
                both = jnp.concatenate([vbuf[head, frame + REACH - back, rows, :], ones], 1)
                product = jnp.dot(weights.astype(jnp.bfloat16), both, preferred_element_type=jnp.float32)
                total = product if top is None else total * jnp.exp2(top - higher) + product
                top = higher
        if end:
            obuf[head, frame] = (total[:, :HEAD_DIM] / total[:, HEAD_DIM:]).astype(jnp.bfloat16)
        else:
            tops[frame] = jnp.broadcast_to(top, (BLOCK, HEAD_DIM))
            totals[frame] = total

    def give_back(head, frame):
        for step in Y_STEPS:
            rows = pl.ds(pl.multiple_of(lax.rem(y + step, RING_Y) * ROWS, ROWS), ROWS)
            pltpu.make_async_remote_copy(
                src_ref=obuf.at[head, frame, rows, :],
                dst_ref=attn.at[frame, :, columns(y, head)],
                send_sem=o_send.at[head],
                recv_sem=o_recv.at[head * FRAMES_HERE + frame],
                device_id=along_y(step),
                device_id_type=MESH,
            ).start()
        rows = pl.ds(pl.multiple_of(y * ROWS, ROWS), ROWS)
        pltpu.make_async_copy(
            obuf.at[head, frame, rows, :],
            attn.at[frame, :, columns(y, head)],
            o_recv.at[head * FRAMES_HERE + frame],
        ).start()

    def compute(head, start, count, roles=ALL, begin=True, end=True):
        def body(frame, carry):
            attend(head, frame, roles, begin, end)
            if end:
                give_back(head, frame)
            return carry

        lax.fori_loop(start, start + count, body, 0)

    def frame_copy(head):
        return pltpu.make_async_remote_copy(
            src_ref=new.at[head],
            dst_ref=incoming.at[head],
            send_sem=f_send.at[head],
            recv_sem=f_recv.at[head],
            device_id=last_group,
            device_id_type=MESH,
        )

    def finish(head, start, count):
        for frame in range(start, start + count):
            wait(attn.at[frame, :, pl.ds(0, PART)], o_recv.at[head * FRAMES_HERE + frame])
            low, high = 2 * frame, 2 * frame + 1
            is_low = level[frame] == group * (2 * FRAMES_HERE) + low
            for owner in range(RING_Y):
                cols = pl.ds((owner * HEADS_HERE + head) * HEAD_DIM, HEAD_DIM)
                pair = gate[:, cols].astype(jnp.float32)
                factor = jnp.where(is_low, step_size[low] * pair[low:high], step_size[high] * pair[high:high + 1])
                result = lat[frame, :, cols].astype(jnp.float32) - factor * attn[frame, :, cols].astype(jnp.float32)
                result = result.astype(jnp.bfloat16)
                attended[frame, :, cols] = attn[frame, :, cols]
                factors[pl.ds(frame, 1), cols] = factor
                if frame == 0:
                    new[head, :, pl.ds(owner * HEAD_DIM, HEAD_DIM)] = result
                else:
                    next_queue[frame - 1, :, cols] = result
            if frame == 0:
                frame_copy(head).start()

    def enter(head):
        frame_copy(head).wait_recv()
        for owner in range(RING_Y):
            cols = pl.ds((owner * HEADS_HERE + head) * HEAD_DIM, HEAD_DIM)
            next_queue[FRAMES_HERE - 1, :, cols] = incoming[head, :, pl.ds(owner * HEAD_DIM, HEAD_DIM)]

    def prepare():
        for copy in local:
            copy.start()

    def prepared():
        for copy in local:
            copy.wait()

    exchange(K, 0)
    exchange(V, 0)
    exchange(K, 1)
    exchange(Q, 0)
    exchange(V, 1)
    exchange(K, 2)
    exchange(Q, 1)
    exchange(V, 2)
    exchange(Q, 2)
    prepare()
    first(K, 0, LATE)
    first(K, 0, EARLY)
    first(V, 0, LATE)
    first(V, 0, EARLY)
    second(K, 0, LATE)
    second(K, 0, EARLY)
    prepared()
    second(V, 0, LATE)
    second(V, 0, EARLY)
    first(K, 1, LATE)
    first(K, 1, EARLY)
    third(K, 0, LATE)
    third(K, 0, EARLY)
    third(V, 0, LATE)
    third(V, 0, EARLY)
    arrive(Q, 0)
    compute(0, 2, 2)
    first(V, 1, LATE)
    first(V, 1, EARLY)
    second(K, 1, LATE)
    second(K, 1, EARLY)
    halo(0, False)
    halo(0, True)
    compute(0, 0, 2)
    second(V, 1, LATE)
    second(V, 1, EARLY)
    third(K, 1, LATE)
    third(K, 1, EARLY)
    first(K, 2, LATE)
    first(K, 2, EARLY)
    third(V, 1, LATE)
    third(V, 1, EARLY)
    arrive(Q, 1)
    compute(1, 2, 2)
    second(K, 2, LATE)
    second(K, 2, EARLY)
    first(V, 2, LATE)
    first(V, 2, EARLY)
    halo(1, False)
    halo(1, True)
    compute(1, 0, 2)
    third(K, 2, LATE)
    third(K, 2, EARLY)
    second(V, 2, LATE)
    second(V, 2, EARLY)
    arrive(Q, 2)
    third(V, 2, LATE)
    third(V, 2, EARLY)
    compute(2, 2, 1)
    halo(2, False)
    halo(2, True)
    compute(2, 0, 2)
    compute(2, 3, 1)
    finish(0, 0, 4)
    finish(1, 0, 4)
    finish(2, 0, 1)
    enter(0)
    enter(1)
    finish(2, 1, 3)
    enter(2)

    away = BLOCK - ROWS
    for head in range(HEADS_HERE):
        frame_copy(head).wait_send()
        for array in (K, V, Q):
            wait(qbuf.at[head, :, pl.ds(0, away), :], y_send.at[array * HEADS_HERE + head])
        for array in (K, V):
            index = array * HEADS_HERE + head
            wait(bufs[array].at[head, pl.ds(0, FRAMES_HERE), pl.ds(0, 3 * BLOCK), :], x_send.at[index])
            wait(bufs[array].at[head, pl.ds(0, REACH)], halo_send.at[index])
        wait(obuf.at[head, :, pl.ds(0, away), :], o_send.at[head])


def per_device(latents, queries, keys, values, levels, reach, gates, steps_table, fresh):
    shape = (FRAMES_HERE, ROWS, WIDTH)
    bf16 = jnp.bfloat16
    hbm = pl.BlockSpec(memory_space=pltpu.HBM)
    vmem = pl.BlockSpec(memory_space=pltpu.VMEM)
    dma = pltpu.SemaphoreType.DMA
    span = (HEADS_HERE, FRAMES_HERE + REACH, FRAME_LEN, HEAD_DIM)
    mine = (HEADS_HERE, FRAMES_HERE, BLOCK, HEAD_DIM)
    attended, queue, factors = pl.pallas_call(
        kernel,
        out_shape=(
            jax.ShapeDtypeStruct(shape, bf16),
            jax.ShapeDtypeStruct(shape, bf16),
            jax.ShapeDtypeStruct((FRAMES_HERE, WIDTH), jnp.float32),
        ),
        in_specs=[hbm] * 8,
        out_specs=(vmem, vmem, vmem),
        scratch_shapes=[
            pltpu.VMEM(span, bf16),
            pltpu.VMEM(span, bf16),
            pltpu.VMEM(mine, bf16),
            pltpu.VMEM(mine, bf16),
            pltpu.VMEM(shape, bf16),
            pltpu.VMEM(shape, bf16),
            pltpu.VMEM((2 * FRAMES_HERE, WIDTH), bf16),
            pltpu.VMEM((HEADS_HERE, ROWS, PART), bf16),
            pltpu.VMEM((HEADS_HERE, ROWS, PART), bf16),
            pltpu.VMEM((FRAMES_HERE, BLOCK, 2 * HEAD_DIM), jnp.float32),
            pltpu.VMEM((FRAMES_HERE, BLOCK, HEAD_DIM), jnp.float32),
            pltpu.SMEM((FRAMES_HERE,), jnp.int32),
            pltpu.SMEM((FRAMES_HERE,), jnp.int32),
            pltpu.SMEM((2 * FRAMES_HERE,), jnp.float32),
            dma((3 * HEADS_HERE,)),
            dma((6 * HEADS_HERE,)),
            dma((2 * HEADS_HERE,)),
            dma((16 * HEADS_HERE,)),
            dma((2 * HEADS_HERE,)),
            dma((4 * HEADS_HERE,)),
            dma((HEADS_HERE,)),
            dma((HEADS_HERE * FRAMES_HERE,)),
            dma((HEADS_HERE,)),
            dma((HEADS_HERE,)),
            dma((5,)),
        ],
        compiler_params=pltpu.CompilerParams(
            collective_id=0, has_side_effects=True, vmem_limit_bytes=62 * 1024 * 1024
        ),
        cost_estimate=pl.CostEstimate(
            flops=9_700_000_000, bytes_accessed=8_000_000, transcendentals=9_500_000
        ),
    )(latents, queries, keys, values, levels, reach, gates, steps_table)
    updated = latents.astype(jnp.float32) - factors[:, None, :] * attended.astype(jnp.float32)
    slot = jnp.arange(FRAMES_HERE, dtype=jnp.int32)[:, None, None]
    is_fresh = (slot == FRAMES_HERE - 1) & (lax.axis_index("frame") == GROUPS - 1)
    return updated.astype(bf16), jnp.where(is_fresh, fresh[None], queue)


def solution(mesh):
    in_specs = (
        P("frame", "tok", None),
        P("frame", "tok", None),
        P("frame", "tok", None),
        P("frame", "tok", None),
        P("frame"),
        P("frame"),
        P("frame", None),
        P("frame"),
        P("tok", None),
    )
    out_specs = (P("frame", "tok", None), P("frame", "tok", None))
    return jax.shard_map(
        per_device, mesh=mesh, in_specs=in_specs, out_specs=out_specs, check_vma=False
    )
```
